32 devices in a mesh: ctx: 8 (over z, y), wa: 4 (over x, core).
Axes of the slice: x: 2, y: 2, z: 4, core: 2. Of those that a mesh axis runs over, the one named last changes fastest.
Arguments:
- inputs: float32 [2048, 2, 768], P('ctx'), may hold values from -6 to 6
- upstream: float32 [2048, 2, 768], P('ctx'), may hold values from -6 to 6
- gain_attn: float32 [768], replicated, may hold values from 0.5 to 1.5
- w_query: bfloat16 [768, 768], P(None, 'wa'), may hold values from -0.078125 to 0.078125
- w_key: bfloat16 [768, 768], P(None, 'wa'), may hold values from -0.078125 to 0.078125
- w_value: bfloat16 [768, 768], P(None, 'wa'), may hold values from -0.21875 to 0.21875
- w_proj: bfloat16 [768, 768], P('wa'), may hold values from -6 to 6
- rel_bias: float32 [32, 12], P(None, 'wa'), may hold values from -4 to 4
- gain_ffn: float32 [768], replicated, may hold values from 0.5 to 1.5
- w_router: bfloat16 [768, 8], replicated, may hold values from -0.15625 to 0.15625
- w_expin: bfloat16 [8, 768, 3072], P('ctx', None, 'wa'), may hold values from -0.21875 to 0.21875
- w_expout: bfloat16 [8, 3072, 768], P('ctx', 'wa'), may hold values from -1.5 to 1.5
- routes: int32 [2048, 2, 1], P('ctx'), may hold values from 0 to 7; in each aligned block of 512 rows (0 to 511, 512 to 1023, ..., all dimensions but the last counted through in order) at most 128 rows name the same one
- bucket_table: int32 [4095], replicated, may hold values from 0 to 31, as said below
Outputs:
- output: float32 [2048, 2, 768], P('ctx')
- grad_inputs: float32 [2048, 2, 768], P('ctx')
- grad_gain_attn: float32 [768], replicated
- grad_w_query: float32 [768, 768], P(None, 'wa')
- grad_w_key: float32 [768, 768], P(None, 'wa')
- grad_w_value: float32 [768, 768], P(None, 'wa')
- grad_w_proj: float32 [768, 768], P('wa')
- grad_rel_bias: float32 [32, 12], P(None, 'wa')
- grad_gain_ffn: float32 [768], replicated
- grad_w_router: float32 [768, 8], replicated
- grad_w_expin: float32 [8, 768, 3072], P('ctx', None, 'wa')
- grad_w_expout: float32 [8, 3072, 768], P('ctx', 'wa')
The draws below stay inside these ranges and needn't reach their ends.
Inputs may be any that keep to these rules, and one draw needn't show every extreme that they name: `routes`: among the 512 tokens of one ctx device (positions of its block, then sequences) at most 128 have the same route, and some route has exactly 128 of them. `bucket_table`: entry r + 2047 is the bucket of a key r positions after its query (before it for negative r); it is 0 at r = 0 and 31 at r = 2047.
All inputs are finite; a program needn't handle non-finite values.
Results may differ from the reference program's by a relative error of at most 0.024.
Values may be sent and summed in bfloat16 or wider, within the bound.
A program may use at most 128 MiB of HBM per device.

```python
import math
import jax
import jax.numpy as jnp
import numpy as np
from jax import lax

D = 768
HEADS = 12
HEAD_DIM = 64
FF = 3072
NB = 32
SEQS = 2
LEN = 2048
TOK_DEV = 512
EXPERTS = 8
CAP = 128
N_CTX = 8


def draw_bucket_table(key, part):
    key = jax.random.fold_in(key, 7)
    half_count = NB // 2
    first_key, second_key = jax.random.split(key)
    offsets = jnp.arange(2 * LEN - 1, dtype=jnp.int32) - (LEN - 1)
    distance = jnp.abs(offsets)

    def cut_points(subkey):
        shuffled = jax.random.permutation(subkey, LEN - 1) + 1
        return shuffled[:half_count - 1].astype(jnp.int32)
    below = cut_points(first_key)
    above = cut_points(second_key)
    count_below = jnp.sum((below[None, :] <= distance[:, None]).astype(jnp.int32), axis=1)
    count_above = jnp.sum((above[None, :] <= distance[:, None]).astype(jnp.int32), axis=1)
    return jnp.where(offsets > 0, half_count + count_above, count_below).astype(jnp.int32)


def level_of(stream_key, dims, pieces, low, top_value):
    loudness = 1.0
    for position, parts in pieces:
        heights = jax.random.uniform(jax.random.fold_in(jax.random.fold_in(stream_key, 6), position), (parts,), jnp.float32, low / len(pieces), top_value / len(pieces))
        loudness = loudness * jnp.repeat(jnp.exp(heights), dims[position] // parts).reshape((-1,) + (1,) * (len(dims) - 1 - position))
    return loudness


def shared_out(key, own, number, rows, count, top, reach, skew):
    order = jax.random.permutation(key, count)
    packed, ordinary = load_shares(count, rows * top, reach, skew, True), load_shares(count, rows * top, reach, skew, False)
    places = jnp.arange(count)

    def named(tallies, turn):
        used = int((tallies > 0).sum())
        fixed = max(1, used // 4)
        passed = fixed + (places - fixed + turn * (used - fixed)) % max(1, count - fixed)
        return jnp.zeros((count,), jnp.int32).at[order[jnp.where(places < fixed, places, passed)]].set(jnp.asarray(tallies, jnp.int32))

    tallies = jnp.where(number % 4 == 0, named(packed, number // 4), named(ordinary, number - number // 4 - 1))
    mixed = jax.random.permutation(jax.random.fold_in(own, 3), count)
    donor, taker = mixed[0:count // 2 * 2:2], mixed[1:count // 2 * 2:2]
    slack = jnp.minimum(tallies[donor] - 1, reach - tallies[taker]) // 2
    slack = jnp.where((donor == order[0]) | (taker == order[0]) | (tallies[taker] == 0), 0, jnp.maximum(slack, 0))
    passed = jax.random.randint(jax.random.fold_in(own, 4), (count // 2,), 0, 1 << 20) % (slack + 1)
    tallies = tallies.at[donor].add(-passed).at[taker].add(passed)
    items = jnp.searchsorted(jnp.cumsum(tallies), jnp.arange(rows * top), side="right").astype(jnp.int32)
    table = items.reshape(top, rows).T
    table = table[jax.random.permutation(jax.random.fold_in(own, 1), rows)]
    turn = jax.random.randint(jax.random.fold_in(own, 2), (rows, 1), 0, top)
    return jnp.take_along_axis(table, (jnp.arange(top)[None, :] + turn) % top, axis=1)


def load_shares(count, total, limit, lean, full):
    loads = [(1 << 20) // math.isqrt(grade ** lean) + 1 for grade in range(1, count + 1)]
    largest = limit if full else min(limit, max(-(-total // count), total * loads[0] // sum(loads)))
    least = 1 if total - largest >= count - 1 else 0
    given, rest = [largest] + [least] * (count - 1), total - largest - least * (count - 1)
    while rest > 0:
        candidates = [i for i in range(1, count) if given[i] < largest] or [i for i in range(1, count) if given[i] < limit]
        whole, remaining = sum([loads[i] for i in candidates]), rest
        for i in candidates:
            extra = min(limit - given[i], max(1, remaining * loads[i] // whole), rest)
            given[i] = given[i] + extra
            rest = rest - extra
    return np.array(given)


def noise(stream_key, dims, spread, most, cuts=(), held_as=jnp.bfloat16):
    entries = spread * jax.random.normal(stream_key, dims, jnp.float32)
    if cuts:
        entries = entries * level_of(stream_key, dims, cuts, -0.22, 0.18)
    return jnp.clip(entries, -most, most).astype(held_as)


def setup_inputs(seed: int = 0) -> dict:
    seeds = jax.random.split(jax.random.key(seed), 15)
    inputs = noise(seeds[0], (LEN, SEQS, D), 1.0, 6.0, ((0, 8),), jnp.float32)
    upstream = noise(seeds[1], (LEN, SEQS, D), 1.0, 6.0, ((0, 8),), jnp.float32)
    gain_attn = jnp.clip(1.0 + 0.1 * jax.random.normal(seeds[2], (D,), jnp.float32), 0.5, 1.5)
    w_query = noise(seeds[3], (D, HEADS * HEAD_DIM), (8 * D) ** -0.5, 0.078125, ((1, 4),))
    w_key = noise(seeds[4], (D, HEADS * HEAD_DIM), (8 * D) ** -0.5, 0.078125, ((1, 4),))
    w_value = noise(seeds[5], (D, HEADS * HEAD_DIM), D ** -0.5, 0.21875, ((1, 4),))
    w_proj = noise(seeds[6], (HEADS * HEAD_DIM, D), ((0.25 * LEN * D ** (0 - 1)) ** 0.5), 6.0, ((0, 4),))
    rel_bias = noise(seeds[7], (NB, HEADS), 0.8, 4.0, ((1, 4),), jnp.float32)
    gain_ffn = jnp.clip(1.0 + 0.1 * jax.random.normal(seeds[8], (D,), jnp.float32), 0.5, 1.5)
    w_router = noise(seeds[9], (D, EXPERTS), (2 * D) ** -0.5, 0.15625)
    w_expin = noise(seeds[10], (EXPERTS, D, FF), D ** -0.5, 0.21875, ((0, 8), (2, 4)))
    w_expout = noise(seeds[11], (EXPERTS, FF, D), (max(1, FF // (3 * EXPERTS * EXPERTS))) ** -0.5, 1.5, ((0, 8), (1, 4)))
    routes_keys = jax.random.split(jax.random.fold_in(seeds[12], 1), LEN * SEQS // TOK_DEV)
    routes_turns = jax.random.permutation(jax.random.fold_in(seeds[12], 3), LEN * SEQS // TOK_DEV)
    routes = jax.vmap(lambda own, number: shared_out(jax.random.fold_in(seeds[12], 2), own, number, TOK_DEV, EXPERTS, 1, CAP, 1))(routes_keys, routes_turns).reshape((LEN, SEQS, 1))
    bucket_table = draw_bucket_table(jax.random.fold_in(seeds[14], 71), 0)
    return {"inputs": inputs, "upstream": upstream, "gain_attn": gain_attn, "w_query": w_query, "w_key": w_key, "w_value": w_value, "w_proj": w_proj, "rel_bias": rel_bias, "gain_ffn": gain_ffn, "w_router": w_router, "w_expin": w_expin, "w_expout": w_expout, "routes": routes, "bucket_table": bucket_table}


@jax.custom_vjp
def low(v):
    return lax.optimization_barrier(v.astype(jnp.bfloat16)).astype(jnp.float32)

@jax.custom_vjp
def low_back(v):
    return v

def low_keep(v):
    return (low(v), None)

def low_pass(kept, grad):
    return (grad,)

def back_keep(v):
    return (v, None)

def back_low(kept, grad):
    return (low(grad),)
low.defvjp(low_keep, low_pass)
low_back.defvjp(back_keep, back_low)
highest = lax.Precision.HIGHEST
eps = 1e-06

def rms_norm(flat_rows, gain):
    return flat_rows * lax.rsqrt(lax.optimization_barrier(jnp.mean(flat_rows * flat_rows, axis=-1, keepdims=True)) + eps) * gain

def gelu_tanh(values):
    return jax.nn.gelu(values, approximate=True)

def attention(query, key_all, value_all, bias_table, bucket_table):
    block_rows = min(512, LEN)
    block_count = LEN // block_rows
    query_seq = jnp.transpose(query, (1, 0, 2, 3)).reshape(SEQS * block_count, block_rows, HEADS, HEAD_DIM)
    key_seq = jnp.transpose(key_all, (1, 0, 2, 3))
    value_seq = jnp.transpose(value_all, (1, 0, 2, 3))

    def one_block(number):
        seq_number = number // block_count
        first_row = number % block_count * block_rows
        query_block = query_seq[number]
        keys_here = key_seq[seq_number]
        values_here = value_seq[seq_number]
        scores = jnp.einsum('qhd,khd->hqk', query_block, keys_here, precision=highest)
        offsets = jnp.arange(LEN, dtype=jnp.int32)[None, :] - (first_row + jnp.arange(block_rows, dtype=jnp.int32))[:, None] + LEN - 1
        bias = jnp.transpose(jnp.take(bias_table, bucket_table[offsets], axis=0), (2, 0, 1))
        scores = low_back(scores + bias)
        row_top = lax.optimization_barrier(jnp.max(scores, axis=-1, keepdims=True))
        log_total = row_top + jnp.log(lax.optimization_barrier(jnp.sum(jnp.exp(scores - row_top), axis=-1, keepdims=True)))
        weights = low(jnp.exp(scores - log_total))
        return jnp.einsum('hqk,khd->qhd', weights, values_here, precision=highest)
    blocks = lax.map(jax.checkpoint(one_block), jnp.arange(SEQS * block_count, dtype=jnp.int32))
    return jnp.transpose(blocks.reshape(SEQS, LEN, HEADS, HEAD_DIM), (1, 0, 2, 3))

def reference(inputs, upstream, gain_attn, w_query, w_key, w_value, w_proj, rel_bias, gain_ffn, w_router, w_expin, w_expout, routes, bucket_table):
    token_total = LEN * SEQS
    route_flat = routes.reshape(token_total)
    expert_ids = jnp.arange(EXPERTS, dtype=jnp.int32)
    chosen = (route_flat[:, None] == expert_ids[None, :]).astype(jnp.int32)
    counts = jnp.cumsum(chosen.reshape(N_CTX, TOK_DEV, EXPERTS), axis=1).reshape(token_total, EXPERTS)
    slot_rank = lax.optimization_barrier(jnp.sum((counts - 1) * chosen, axis=1))
    owner = jnp.arange(token_total, dtype=jnp.int32) // TOK_DEV
    destination = route_flat * (N_CTX * CAP) + owner * CAP + slot_rank
    chosen_float = chosen.astype(jnp.float32)

    def layer(layer_in, gain_one, query_weight, key_weight, value_weight, proj_weight, bias_table, gain_two, router_weight, expin_weight, expout_weight):
        flat_rows = layer_in.reshape(token_total, D)
        normed1_low = low(rms_norm(flat_rows, gain_one))

        def project(weight):
            return low(low_back(jnp.dot(normed1_low, weight, precision=highest))).reshape(LEN, SEQS, HEADS, HEAD_DIM)
        attended = attention(project(query_weight), project(key_weight), project(value_weight), bias_table, bucket_table)
        attended_low = low(low_back(attended.reshape(token_total, HEADS * HEAD_DIM)))
        attn_out = low_back(jnp.dot(attended_low, proj_weight, precision=highest))
        hidden1 = flat_rows + attn_out
        normed2_low = low(rms_norm(hidden1, gain_two))
        router_prob = jax.nn.softmax(jnp.dot(normed2_low, router_weight, precision=highest), axis=-1)
        gate_value = lax.optimization_barrier(jnp.sum(router_prob * chosen_float, axis=1))
        slots = jnp.zeros((EXPERTS * N_CTX * CAP, D), jnp.float32).at[destination].set(normed2_low)
        slots = slots.reshape(EXPERTS, N_CTX * CAP, D)

        def one_expert(operands):
            expert_rows, first_weight, second_weight = operands
            pre_act = low_back(jnp.dot(expert_rows, first_weight, precision=highest))
            return jnp.dot(low(gelu_tanh(pre_act)), second_weight, precision=highest)
        expert_result = lax.map(jax.checkpoint(one_expert), (slots, expin_weight, expout_weight))
        expert_out = low_back(expert_result.reshape(EXPERTS * N_CTX * CAP, D)[destination])
        return (hidden1 + gate_value[:, None] * expert_out).reshape(LEN, SEQS, D)
    output, pullback = jax.vjp(layer, inputs.astype(jnp.float32), gain_attn.astype(jnp.float32), w_query.astype(jnp.float32), w_key.astype(jnp.float32), w_value.astype(jnp.float32), w_proj.astype(jnp.float32), rel_bias.astype(jnp.float32), gain_ffn.astype(jnp.float32), w_router.astype(jnp.float32), w_expin.astype(jnp.float32), w_expout.astype(jnp.float32))
    grads = pullback(upstream.astype(jnp.float32))
    return (output, grads[0], grads[1], grads[2], grads[3], grads[4], grads[5], grads[6], grads[7], grads[8], grads[9], grads[10])
```

```python
import functools

import jax
import jax.numpy as jnp
from jax import lax
from jax.experimental import pallas as pl
from jax.experimental.pallas import tpu as pltpu
from jax.sharding import PartitionSpec as P

eps = 1e-06
highest = lax.Precision.HIGHEST


def gelu_tanh(values):
    return jax.nn.gelu(values, approximate=True)


def rms_forward(flat_rows, gain):
    scale = lax.rsqrt(jnp.mean(flat_rows * flat_rows, axis=-1, keepdims=True) + eps)
    return (flat_rows * scale * gain, scale)


def rms_backward(flat_rows, scale, gain, grad_out):
    weighted = grad_out * gain
    inner_mean = jnp.mean(weighted * flat_rows, axis=-1, keepdims=True)
    grad_rows = scale * weighted - flat_rows * scale * scale * scale * inner_mean
    grad_gain = jnp.sum(grad_out * flat_rows * scale, axis=0)
    return (grad_rows, grad_gain)


def spread_bias(base, wide_ref):
    rows = base.shape[0]
    wide_ref[0:rows, :] = base
    while rows < wide_ref.shape[0]:
        wide_ref[rows : 2 * rows, :] = pltpu.roll(wide_ref[0:rows, :], rows, 1)
        rows = 2 * rows


def fold_diagonals(wide_ref):
    rows, width = wide_ref.shape
    while rows > 8:
        rows = rows // 2
        moved = pltpu.roll(wide_ref[rows : 2 * rows, :], width - rows, 1)
        wide_ref[0:rows, :] = wide_ref[0:rows, :] + moved
    return wide_ref[0:8, :]


def over_blocks(count, init, step):
    group = 8 if count % 8 == 0 else 1

    def some(turn, state):
        for inner in range(group):
            state = step(turn * group + inner, state)
        return state

    if count == group:
        return some(0, init)
    return lax.fori_loop(0, count // group, some, init)


def nt_dot(left, right):
    return lax.dot_general(left, right, (((1,), (1,)), ((), ())), preferred_element_type=jnp.float32)


def lanes(number, width):
    start = number * width
    return pl.ds(start if isinstance(start, int) else pl.multiple_of(start, width), width)


def attend_kernel(head_dim, base_ref, query_ref, kv_ref, out_ref, lse_ref, wide_ref, score_ref):
    heads = base_ref.shape[0]
    blocks, head_rows, tokens = kv_ref.shape
    block = wide_ref.shape[0]
    seqs = tokens // block
    for head in range(heads):
        spread_bias(base_ref[head], wide_ref)
        key_at = slice(head * head_dim, (head + 1) * head_dim)
        value_at = slice(head_rows // 2 + head * head_dim, head_rows // 2 + (head + 1) * head_dim)
        for seq in range(seqs):
            here = slice(seq * block, (seq + 1) * block)
            query = query_ref[here, key_at]

            def score_step(number, top):
                scores = jnp.dot(query, kv_ref[number, key_at, here], preferred_element_type=jnp.float32)
                scores = scores + wide_ref[:, lanes(number, block)]
                score_ref[number] = scores
                return jnp.maximum(top, scores)

            top = over_blocks(blocks, jnp.full((block, block), -3e38, jnp.float32), score_step)
            top = jnp.max(top, axis=1, keepdims=True)

            def value_step(number, state):
                mass, total = state
                weights = jnp.exp(score_ref[number] - top)
                total = total + nt_dot(weights.astype(jnp.bfloat16), kv_ref[number, value_at, here])
                return (mass + weights, total)

            mass, total = over_blocks(
                blocks,
                (jnp.zeros((block, block), jnp.float32), jnp.zeros((block, head_dim), jnp.float32)),
                value_step,
            )
            mass = jnp.sum(mass, axis=1, keepdims=True)
            out_ref[here, key_at] = total / mass
            lse_ref[head, here, :] = top + jnp.log(mass)


def attend_back_kernel(
    head_dim,
    base_ref,
    query_ref,
    query_t_ref,
    grad_ref,
    grad_t_ref,
    out_ref,
    lse_ref,
    kv_ref,
    dquery_ref,
    dkv_ref,
    dline_ref,
    wide_ref,
    fold_ref,
):
    heads = base_ref.shape[0]
    blocks, head_rows, tokens = kv_ref.shape
    block = wide_ref.shape[0]
    seqs = tokens // block
    for head in range(heads):
        spread_bias(base_ref[head], wide_ref)
        key_at = slice(head * head_dim, (head + 1) * head_dim)
        value_at = slice(head_rows // 2 + head * head_dim, head_rows // 2 + (head + 1) * head_dim)
        deltas = [
            jnp.sum(
                grad_ref[seq * block : (seq + 1) * block, key_at].astype(jnp.float32)
                * out_ref[seq * block : (seq + 1) * block, key_at],
                axis=1,
                keepdims=True,
            )
            for seq in range(seqs)
        ]

        def step(number, state):
            bias = wide_ref[:, lanes(number, block)]
            new_state, seen = [], None
            for seq in range(seqs):
                here = slice(seq * block, (seq + 1) * block)
                key_t = kv_ref[number, key_at, here]
                scores = jnp.dot(query_ref[here, key_at], key_t, preferred_element_type=jnp.float32)
                weights = jnp.exp(scores + bias - lse_ref[head, here, :])
                grad_weights = jnp.dot(
                    grad_ref[here, key_at],
                    kv_ref[number, value_at, here],
                    preferred_element_type=jnp.float32,
                )
                grad_scores = (weights * (grad_weights - deltas[seq])).astype(jnp.bfloat16)
                dkv_ref[number, key_at, here] = jnp.dot(
                    query_t_ref[key_at, here], grad_scores, preferred_element_type=jnp.float32
                ).astype(jnp.bfloat16)
                dkv_ref[number, value_at, here] = jnp.dot(
                    grad_t_ref[key_at, here],
                    weights.astype(jnp.bfloat16),
                    preferred_element_type=jnp.float32,
                ).astype(jnp.bfloat16)
                new_state.append(state[seq] + nt_dot(grad_scores, key_t))
                wide = grad_scores.astype(jnp.float32)
                seen = wide if seen is None else seen + wide
            fold_ref[:, lanes(number, block)] = seen
            return tuple(new_state)

        totals = over_blocks(
            blocks, tuple(jnp.zeros((block, head_dim), jnp.float32) for _ in range(seqs)), step
        )
        for seq in range(seqs):
            dquery_ref[seq * block : (seq + 1) * block, key_at] = totals[seq]
        fold_ref[:, blocks * block :] = jnp.zeros((block, block), jnp.float32)
        dline_ref[head] = fold_diagonals(fold_ref)


def in_vmem(count):
    return [pl.BlockSpec(memory_space=pltpu.VMEM)] * count


params = pltpu.CompilerParams(vmem_limit_bytes=58 * 1024 * 1024)


def attend(base, query, kv_all, head_dim):
    heads, _, width = base.shape
    blocks, _, tokens = kv_all.shape
    block = width // (blocks + 1)
    return pl.pallas_call(
        functools.partial(attend_kernel, head_dim),
        out_shape=(
            jax.ShapeDtypeStruct(query.shape, jnp.float32),
            jax.ShapeDtypeStruct((heads, tokens, 1), jnp.float32),
        ),
        in_specs=in_vmem(3),
        out_specs=tuple(in_vmem(2)),
        scratch_shapes=[
            pltpu.VMEM((block, width), jnp.float32),
            pltpu.VMEM((blocks, block, block), jnp.float32),
        ],
        compiler_params=params,
    )(base, query, kv_all)


def attend_back(base, query, query_t, grad, grad_t, attended, lse, kv_all, head_dim):
    heads, _, width = base.shape
    blocks = kv_all.shape[0]
    block = width // (blocks + 1)
    return pl.pallas_call(
        functools.partial(attend_back_kernel, head_dim),
        out_shape=(
            jax.ShapeDtypeStruct(query.shape, jnp.float32),
            jax.ShapeDtypeStruct(kv_all.shape, jnp.bfloat16),
            jax.ShapeDtypeStruct(base.shape, jnp.float32),
        ),
        in_specs=in_vmem(8),
        out_specs=tuple(in_vmem(3)),
        scratch_shapes=[
            pltpu.VMEM((block, width), jnp.float32),
            pltpu.VMEM((block, width), jnp.float32),
        ],
        compiler_params=params,
    )(base, query, query_t, grad, grad_t, attended, lse, kv_all)


def f32_dot(spec, left, right):
    return jnp.einsum(spec, left, right, preferred_element_type=jnp.float32)


def low(values):
    return values.astype(jnp.bfloat16)


def body(
    inputs,
    upstream,
    gain_attn,
    w_query,
    w_key,
    w_value,
    w_proj,
    rel_bias,
    gain_ffn,
    w_router,
    w_expin,
    w_expout,
    routes,
    bucket_table,
):
    block_len, seq_count, model_width = inputs.shape
    ctx_size = lax.axis_size("ctx")
    wa_size = lax.axis_size("wa")
    seq_len = block_len * ctx_size
    tok_count = block_len * seq_count
    head_local = rel_bias.shape[1]
    head_cols = w_query.shape[1]
    head_dim = head_cols // head_local
    bucket_count = rel_bias.shape[0]
    expert_count = w_router.shape[1]
    capacity = 2 * tok_count // expert_count
    my_index = lax.axis_index("ctx")
    wa_index = lax.axis_index("wa")

    def by_sequence(rows):
        return jnp.transpose(rows, (1, 0, 2)).reshape(tok_count, rows.shape[2])

    def by_position(rows):
        return jnp.transpose(rows.reshape(seq_count, block_len, model_width), (1, 0, 2))

    flat_rows = by_sequence(inputs)
    grad_rows = by_sequence(upstream)
    normed1, scale1 = rms_forward(flat_rows, gain_attn)
    normed1_low = low(normed1)
    w_kv = jnp.concatenate([w_key, w_value], axis=1)
    kv_t = low(f32_dot("ck,tc->kt", w_kv, normed1_low))
    kv_all = lax.all_gather(kv_t, "ctx", axis=0)
    query_low = low(f32_dot("tc,ck->tk", normed1_low, w_query))
    query_t = query_low.T

    width = seq_len + block_len
    window = lax.dynamic_slice_in_dim(
        jnp.pad(bucket_table, (0, 1)), seq_len - block_len - my_index * block_len, width
    )
    bucket_ids = jnp.arange(bucket_count, dtype=jnp.int32)
    in_bucket = (window[None, :] == bucket_ids[:, None]).astype(jnp.float32)
    line = jnp.einsum("bh,bj->hj", rel_bias, in_bucket, precision=highest)
    base = jnp.stack([jnp.roll(line, row - (block_len - 1), axis=1) for row in range(8)], axis=1)

    route_flat = by_sequence(routes).reshape(tok_count)
    expert_ids = jnp.arange(expert_count, dtype=jnp.int32)
    chosen = route_flat[:, None] == expert_ids[None, :]
    chosen_float = chosen.astype(jnp.float32)
    token_ids = jnp.arange(tok_count, dtype=jnp.int32)
    earlier = low(token_ids[:, None] > token_ids[None, :])
    ranks = f32_dot("tu,ue->te", earlier, low(chosen_float))
    slot_rank = jnp.sum(ranks * chosen_float, axis=1).astype(jnp.int32)
    part_cap = capacity // wa_size
    part_rows = expert_count * part_cap
    slot_index = (slot_rank // part_cap) * part_rows + route_flat * part_cap + slot_rank % part_cap
    own_slots = wa_index * part_rows + jnp.arange(part_rows, dtype=jnp.int32)
    dispatch = low(own_slots[:, None] == slot_index[None, :])
    all_slots = jnp.arange(wa_size * part_rows, dtype=jnp.int32)
    combine = low(slot_index[:, None] == all_slots[None, :])

    attended, lse = attend(base, query_low, kv_all, head_dim)
    attended_low = low(attended)
    attn_share = f32_dot("tk,kd->td", attended_low, w_proj)
    attn_out = lax.psum(low(attn_share), "wa").astype(jnp.float32)
    hidden1 = flat_rows + attn_out
    normed2, scale2 = rms_forward(hidden1, gain_ffn)
    normed2_low = low(normed2)
    logits = f32_dot("td,de->te", normed2_low, w_router)
    router_prob = jax.nn.softmax(logits, axis=-1)
    gate_value = jnp.sum(router_prob * chosen_float, axis=1)
    grad_expert = low(gate_value[:, None] * grad_rows)

    both = jnp.concatenate([normed2_low, grad_expert], axis=1)
    packed = low(f32_dot("st,td->sd", dispatch, both))
    landed = lax.all_to_all(packed, "ctx", split_axis=0, concat_axis=0, tiled=True)
    rows_in = lax.all_gather(landed, "wa", axis=0, tiled=True)
    received = rows_in[:, :model_width]
    grad_received = rows_in[:, model_width:]
    w_in, w_out = w_expin[0], w_expout[0]
    pre_act = f32_dot("rd,df->rf", received, w_in)
    activated, gelu_back = jax.vjp(gelu_tanh, pre_act)
    activated_low = low(activated)
    expert_part = f32_dot("rf,fd->rd", activated_low, w_out)
    grad_act = f32_dot("rd,fd->rf", grad_received, w_out)
    grad_pre = low(gelu_back(grad_act)[0])
    grad_inpart = f32_dot("rf,df->rd", grad_pre, w_in)
    rows_out = jnp.concatenate([low(expert_part), low(grad_inpart)], axis=1)
    summed_part = lax.psum_scatter(rows_out, "wa", scatter_dimension=0, tiled=True)
    returned = lax.all_to_all(summed_part, "ctx", split_axis=0, concat_axis=0, tiled=True)
    slot_rows = lax.all_gather(returned, "wa", axis=0, tiled=True)
    grad_wout = f32_dot("rf,rd->fd", activated_low, grad_received)[None]
    grad_win = f32_dot("rd,rf->df", received, grad_pre)[None]
    token_rows = f32_dot("ts,sd->td", combine, slot_rows)
    expert_out = token_rows[:, :model_width]
    grad_from_experts = token_rows[:, model_width:]

    output_rows = hidden1 + gate_value[:, None] * expert_out
    grad_gate = jnp.sum(grad_rows * expert_out, axis=1)
    grad_logits = router_prob * (chosen_float - gate_value[:, None]) * grad_gate[:, None]
    router_float = w_router.astype(jnp.float32)
    grad_normed2 = grad_from_experts + jnp.einsum(
        "te,de->td", grad_logits, router_float, precision=highest
    )
    grad_router = jnp.einsum(
        "td,te->de", normed2_low.astype(jnp.float32), grad_logits, precision=highest
    )
    grad_norm2_in, grad_gain2 = rms_backward(hidden1, scale2, gain_ffn, grad_normed2)
    grad_hidden1 = grad_rows + grad_norm2_in
    grad_attn_low = low(grad_hidden1)
    grad_proj = f32_dot("tk,td->kd", attended_low, grad_attn_low)
    grad_attended = low(f32_dot("td,kd->tk", grad_attn_low, w_proj))
    dquery, dkv, dline = attend_back(
        base,
        query_low,
        query_t,
        grad_attended,
        grad_attended.T,
        attended,
        lse,
        kv_all,
        head_dim,
    )
    dkv_t = lax.psum_scatter(dkv, "ctx", scatter_dimension=0)
    folded = sum(jnp.roll(dline[:, row, :], block_len - 1 - row, axis=1) for row in range(8))
    grad_bias = jnp.einsum("bj,hj->bh", in_bucket, folded, precision=highest)
    dquery_low = low(dquery)
    grad_wq = f32_dot("tc,tk->ck", normed1_low, dquery_low)
    grad_wkv = f32_dot("tc,kt->ck", normed1_low, dkv_t)
    grad_normed1_part = f32_dot("tk,ck->tc", dquery_low, w_query) + f32_dot(
        "kt,ck->tc", dkv_t, w_kv
    )
    grad_normed1 = lax.psum(low(grad_normed1_part), "wa").astype(jnp.float32)
    grad_norm1_in, grad_gain1 = rms_backward(flat_rows, scale1, gain_attn, grad_normed1)
    grad_inputs = grad_hidden1 + grad_norm1_in

    def over_ctx(values):
        return lax.psum(low(values), "ctx").astype(jnp.float32)

    sum_proj = over_ctx(grad_proj)
    sum_router = over_ctx(grad_router)
    sum_gain2 = over_ctx(grad_gain2)
    sum_wq = over_ctx(grad_wq)
    sum_bias = over_ctx(grad_bias)
    sum_wkv = over_ctx(grad_wkv)
    sum_gain1 = over_ctx(grad_gain1)
    return (
        by_position(output_rows),
        by_position(grad_inputs),
        sum_gain1,
        sum_wq,
        sum_wkv[:, :head_cols],
        sum_wkv[:, head_cols:],
        sum_proj,
        sum_bias,
        sum_gain2,
        sum_router,
        grad_win,
        grad_wout,
    )


def solution(mesh):
    in_specs = (
        P("ctx", None, None),
        P("ctx", None, None),
        P(),
        P(None, "wa"),
        P(None, "wa"),
        P(None, "wa"),
        P("wa", None),
        P(None, "wa"),
        P(),
        P(),
        P("ctx", None, "wa"),
        P("ctx", "wa", None),
        P("ctx", None, None),
        P(),
    )
    out_specs = (
        P("ctx", None, None),
        P("ctx", None, None),
        P(),
        P(None, "wa"),
        P(None, "wa"),
        P(None, "wa"),
        P("wa", None),
        P(None, "wa"),
        P(),
        P(),
        P("ctx", None, "wa"),
        P("ctx", "wa", None),
    )
    return jax.shard_map(body, mesh=mesh, in_specs=in_specs, out_specs=out_specs, check_vma=False)
```

```python
import functools

import jax
import jax.numpy as jnp
from jax import lax
from jax.experimental import pallas as pl
from jax.experimental.pallas import tpu as pltpu
from jax.sharding import PartitionSpec as P

eps = 1e-06
highest = lax.Precision.HIGHEST


def gelu_tanh(values):
    return jax.nn.gelu(values, approximate=True)


def rms_forward(flat_rows, gain):
    scale = lax.rsqrt(jnp.mean(flat_rows * flat_rows, axis=-1, keepdims=True) + eps)
    return (flat_rows * scale * gain, scale)


def rms_backward(flat_rows, scale, gain, grad_out):
    weighted = grad_out * gain
    inner_mean = jnp.mean(weighted * flat_rows, axis=-1, keepdims=True)
    grad_rows = scale * weighted - flat_rows * scale * scale * scale * inner_mean
    grad_gain = jnp.sum(grad_out * flat_rows * scale, axis=0)
    return (grad_rows, grad_gain)


def spread_bias(base, wide_ref):
    rows = base.shape[0]
    wide_ref[0:rows, :] = base
    while rows < wide_ref.shape[0]:
        wide_ref[rows : 2 * rows, :] = pltpu.roll(wide_ref[0:rows, :], rows, 1)
        rows = 2 * rows


def fold_diagonals(wide_ref):
    rows, width = wide_ref.shape
    while rows > 8:
        rows = rows // 2
        moved = pltpu.roll(wide_ref[rows : 2 * rows, :], width - rows, 1)
        wide_ref[0:rows, :] = wide_ref[0:rows, :] + moved
    return wide_ref[0:8, :]


def over_blocks(count, init, step):
    group = 8 if count % 8 == 0 else 1

    def some(turn, state):
        for inner in range(group):
            state = step(turn * group + inner, state)
        return state

    if count == group:
        return some(0, init)
    return lax.fori_loop(0, count // group, some, init)


def nt_dot(left, right):
    return lax.dot_general(left, right, (((1,), (1,)), ((), ())), preferred_element_type=jnp.float32)


def lanes(number, width):
    start = number * width
    return pl.ds(start if isinstance(start, int) else pl.multiple_of(start, width), width)


def attend_kernel(head_dim, base_ref, query_ref, kv_ref, out_ref, lse_ref, wide_ref, score_ref):
    heads = base_ref.shape[0]
    blocks, head_rows, tokens = kv_ref.shape
    block = wide_ref.shape[0]
    seqs = tokens // block
    for head in range(heads):
        spread_bias(base_ref[head], wide_ref)
        key_at = slice(head * head_dim, (head + 1) * head_dim)
        value_at = slice(head_rows // 2 + head * head_dim, head_rows // 2 + (head + 1) * head_dim)
        for seq in range(seqs):
            here = slice(seq * block, (seq + 1) * block)
            query = query_ref[here, key_at]

            def score_step(number, top):
                scores = jnp.dot(query, kv_ref[number, key_at, here], preferred_element_type=jnp.float32)
                scores = scores + wide_ref[:, lanes(number, block)]
                score_ref[number] = scores
                return jnp.maximum(top, scores)

            top = over_blocks(blocks, jnp.full((block, block), -3e38, jnp.float32), score_step)
            top = jnp.max(top, axis=1, keepdims=True)

            def value_step(number, state):
                mass, total = state
                weights = jnp.exp(score_ref[number] - top)
                total = total + nt_dot(weights.astype(jnp.bfloat16), kv_ref[number, value_at, here])
                return (mass + weights, total)

            mass, total = over_blocks(
                blocks,
                (jnp.zeros((block, block), jnp.float32), jnp.zeros((block, head_dim), jnp.float32)),
                value_step,
            )
            mass = jnp.sum(mass, axis=1, keepdims=True)
            out_ref[here, key_at] = total / mass
            lse_ref[head, here, :] = top + jnp.log(mass)


def attend_back_kernel(
    head_dim,
    base_ref,
    query_ref,
    grad_ref,
    out_ref,
    lse_ref,
    kv_ref,
    dquery_ref,
    dline_ref,
    wide_ref,
    fold_ref,
):
    heads = base_ref.shape[0]
    blocks, head_rows, tokens = kv_ref.shape
    block = wide_ref.shape[0]
    seqs = tokens // block
    for head in range(heads):
        spread_bias(base_ref[head], wide_ref)
        key_at = slice(head * head_dim, (head + 1) * head_dim)
        value_at = slice(head_rows // 2 + head * head_dim, head_rows // 2 + (head + 1) * head_dim)
        deltas = [
            jnp.sum(
                grad_ref[seq * block : (seq + 1) * block, key_at].astype(jnp.float32)
                * out_ref[seq * block : (seq + 1) * block, key_at],
                axis=1,
                keepdims=True,
            )
            for seq in range(seqs)
        ]

        def step(number, state):
            bias = wide_ref[:, lanes(number, block)]
            new_state, seen = [], None
            for seq in range(seqs):
                here = slice(seq * block, (seq + 1) * block)
                key_t = kv_ref[number, key_at, here]
                scores = jnp.dot(query_ref[here, key_at], key_t, preferred_element_type=jnp.float32)
                weights = jnp.exp(scores + bias - lse_ref[head, here, :])
                grad_weights = jnp.dot(
                    grad_ref[here, key_at],
                    kv_ref[number, value_at, here],
                    preferred_element_type=jnp.float32,
                )
                grad_scores = (weights * (grad_weights - deltas[seq])).astype(jnp.bfloat16)
                new_state.append(state[seq] + nt_dot(grad_scores, key_t))
                wide = grad_scores.astype(jnp.float32)
                seen = wide if seen is None else seen + wide
            fold_ref[:, lanes(number, block)] = seen
            return tuple(new_state)

        totals = over_blocks(
            blocks, tuple(jnp.zeros((block, head_dim), jnp.float32) for _ in range(seqs)), step
        )
        for seq in range(seqs):
            dquery_ref[seq * block : (seq + 1) * block, key_at] = totals[seq]
        fold_ref[:, blocks * block :] = jnp.zeros((block, block), jnp.float32)
        dline_ref[head] = fold_diagonals(fold_ref)


def stat_row(ref, number, first, here, head, heads):
    held = ref[number, first : first + 16, here].astype(jnp.float32)
    return sum(held[part * heads + head : part * heads + head + 1, :] for part in range(3))


def key_back_kernel(
    head_dim, base_ref, key_ref, value_ref, query_ref, grad_ref, dkey_ref, dvalue_ref, wide_ref
):
    heads = base_ref.shape[0]
    blocks, _, tokens = query_ref.shape
    block = wide_ref.shape[0]
    seqs = tokens // block
    for head in range(heads):
        spread_bias(base_ref[head], wide_ref)
        head_at = slice(head * head_dim, (head + 1) * head_dim)

        def step(number, state):
            bias = wide_ref[:, lanes(number, block)]
            new_state = []
            for seq in range(seqs):
                here = slice(seq * block, (seq + 1) * block)
                query_t = query_ref[number, head_at, here]
                grad_t = grad_ref[number, head_at, here]
                lse = stat_row(query_ref, number, heads * head_dim, here, head, heads)
                delta = stat_row(grad_ref, number, heads * head_dim, here, head, heads)
                scores = jnp.dot(key_ref[here, head_at], query_t, preferred_element_type=jnp.float32)
                weights = jnp.exp(scores + bias - lse)
                grad_weights = jnp.dot(
                    value_ref[here, head_at], grad_t, preferred_element_type=jnp.float32
                )
                grad_scores = (weights * (grad_weights - delta)).astype(jnp.bfloat16)
                dkey, dvalue = state[seq]
                new_state.append(
                    (
                        dkey + nt_dot(grad_scores, query_t),
                        dvalue + nt_dot(weights.astype(jnp.bfloat16), grad_t),
                    )
                )
            return tuple(new_state)

        zero = jnp.zeros((block, head_dim), jnp.float32)
        totals = over_blocks(blocks, tuple((zero, zero) for _ in range(seqs)), step)
        for seq in range(seqs):
            here = slice(seq * block, (seq + 1) * block)
            dkey_ref[here, head_at] = totals[seq][0]
            dvalue_ref[here, head_at] = totals[seq][1]


def in_vmem(count):
    return [pl.BlockSpec(memory_space=pltpu.VMEM)] * count


params = pltpu.CompilerParams(vmem_limit_bytes=58 * 1024 * 1024)


def attend(base, query, kv_all, head_dim):
    heads, _, width = base.shape
    blocks, _, tokens = kv_all.shape
    block = width // (blocks + 1)
    return pl.pallas_call(
        functools.partial(attend_kernel, head_dim),
        out_shape=(
            jax.ShapeDtypeStruct(query.shape, jnp.float32),
            jax.ShapeDtypeStruct((heads, tokens, 1), jnp.float32),
        ),
        in_specs=in_vmem(3),
        out_specs=tuple(in_vmem(2)),
        scratch_shapes=[
            pltpu.VMEM((block, width), jnp.float32),
            pltpu.VMEM((blocks, block, block), jnp.float32),
        ],
        compiler_params=params,
    )(base, query, kv_all)


def attend_back(base, query, grad, attended, lse, kv_all, head_dim):
    heads, _, width = base.shape
    blocks = kv_all.shape[0]
    block = width // (blocks + 1)
    return pl.pallas_call(
        functools.partial(attend_back_kernel, head_dim),
        out_shape=(
            jax.ShapeDtypeStruct(query.shape, jnp.float32),
            jax.ShapeDtypeStruct(base.shape, jnp.float32),
        ),
        in_specs=in_vmem(6),
        out_specs=tuple(in_vmem(2)),
        scratch_shapes=[
            pltpu.VMEM((block, width), jnp.float32),
            pltpu.VMEM((block, width), jnp.float32),
        ],
        compiler_params=params,
        cost_estimate=pl.CostEstimate(
            flops=3 * 2 * query.size * (width - block), bytes_accessed=40_000_000, transcendentals=0
        ),
    )(base, query, grad, attended, lse, kv_all)


def key_back(base, keys, values, query_all, grad_all, head_dim):
    _, _, width = base.shape
    block = width // (query_all.shape[0] + 1)
    shape = jax.ShapeDtypeStruct(keys.shape, jnp.float32)
    return pl.pallas_call(
        functools.partial(key_back_kernel, head_dim),
        out_shape=(shape, shape),
        in_specs=in_vmem(5),
        out_specs=tuple(in_vmem(2)),
        scratch_shapes=[pltpu.VMEM((block, width), jnp.float32)],
        compiler_params=params,
    )(base, keys, values, query_all, grad_all)


def with_stats(rows_t, stats):
    parts, rest = [], stats
    for _ in range(3):
        top = lax.reduce_precision(rest, 8, 7)
        parts.append(low(top))
        rest = rest - top
    parts.append(jnp.zeros((16 - 3 * stats.shape[0], stats.shape[1]), jnp.bfloat16))
    return jnp.concatenate([rows_t] + parts, axis=0)


def f32_dot(spec, left, right):
    return jnp.einsum(spec, left, right, preferred_element_type=jnp.float32)


def low(values):
    return values.astype(jnp.bfloat16)


def body(
    inputs,
    upstream,
    gain_attn,
    w_query,
    w_key,
    w_value,
    w_proj,
    rel_bias,
    gain_ffn,
    w_router,
    w_expin,
    w_expout,
    routes,
    bucket_table,
):
    block_len, seq_count, model_width = inputs.shape
    ctx_size = lax.axis_size("ctx")
    wa_size = lax.axis_size("wa")
    seq_len = block_len * ctx_size
    tok_count = block_len * seq_count
    head_local = rel_bias.shape[1]
    head_cols = w_query.shape[1]
    head_dim = head_cols // head_local
    bucket_count = rel_bias.shape[0]
    expert_count = w_router.shape[1]
    capacity = 2 * tok_count // expert_count
    my_index = lax.axis_index("ctx")
    wa_index = lax.axis_index("wa")

    def by_sequence(rows):
        return jnp.transpose(rows, (1, 0, 2)).reshape(tok_count, rows.shape[2])

    def by_position(rows):
        return jnp.transpose(rows.reshape(seq_count, block_len, model_width), (1, 0, 2))

    flat_rows = by_sequence(inputs)
    grad_rows = by_sequence(upstream)
    normed1, scale1 = rms_forward(flat_rows, gain_attn)
    normed1_low = low(normed1)
    w_kv = jnp.concatenate([w_key, w_value], axis=1)
    kv_t = low(f32_dot("ck,tc->kt", w_kv, normed1_low))
    kv_all = lax.all_gather(kv_t, "ctx", axis=0)
    query_low = low(f32_dot("tc,ck->tk", normed1_low, w_query))
    key_low, value_low = kv_t[:head_cols].T, kv_t[head_cols:].T

    width = seq_len + block_len
    bucket_ids = jnp.arange(bucket_count, dtype=jnp.int32)

    def bias_base(table):
        window = lax.dynamic_slice_in_dim(
            jnp.pad(table, (0, 1)), seq_len - block_len - my_index * block_len, width
        )
        in_bucket = (window[None, :] == bucket_ids[:, None]).astype(jnp.float32)
        line = jnp.einsum("bh,bj->hj", rel_bias, in_bucket, precision=highest)
        rows = [jnp.roll(line, row - (block_len - 1), axis=1) for row in range(8)]
        return jnp.stack(rows, axis=1), in_bucket

    base, in_bucket = bias_base(bucket_table)
    base_t, _ = bias_base(bucket_table[::-1])

    route_flat = by_sequence(routes).reshape(tok_count)
    expert_ids = jnp.arange(expert_count, dtype=jnp.int32)
    chosen = route_flat[:, None] == expert_ids[None, :]
    chosen_float = chosen.astype(jnp.float32)
    token_ids = jnp.arange(tok_count, dtype=jnp.int32)
    earlier = low(token_ids[:, None] > token_ids[None, :])
    ranks = f32_dot("tu,ue->te", earlier, low(chosen_float))
    slot_rank = jnp.sum(ranks * chosen_float, axis=1).astype(jnp.int32)
    part_cap = capacity // wa_size
    part_rows = expert_count * part_cap
    slot_index = (slot_rank // part_cap) * part_rows + route_flat * part_cap + slot_rank % part_cap
    own_slots = wa_index * part_rows + jnp.arange(part_rows, dtype=jnp.int32)
    dispatch = low(own_slots[:, None] == slot_index[None, :])
    all_slots = jnp.arange(wa_size * part_rows, dtype=jnp.int32)
    combine = low(slot_index[:, None] == all_slots[None, :])

    attended, lse = attend(base, query_low, kv_all, head_dim)
    attended_low = low(attended)
    attn_share = f32_dot("tk,kd->td", attended_low, w_proj)
    attn_out = lax.psum(low(attn_share), "wa").astype(jnp.float32)
    query_pack = with_stats(query_low.T, lse[:, :, 0])
    query_pack, attn_out = lax.optimization_barrier((query_pack, attn_out))
    query_all = lax.all_gather(query_pack, "ctx", axis=0)
    hidden1 = flat_rows + attn_out
    normed2, scale2 = rms_forward(hidden1, gain_ffn)
    normed2_low = low(normed2)
    logits = f32_dot("td,de->te", normed2_low, w_router)
    router_prob = jax.nn.softmax(logits, axis=-1)
    gate_value = jnp.sum(router_prob * chosen_float, axis=1)
    grad_expert = low(gate_value[:, None] * grad_rows)

    both = jnp.concatenate([normed2_low, grad_expert], axis=1)
    packed = low(f32_dot("st,td->sd", dispatch, both))
    landed = lax.all_to_all(packed, "ctx", split_axis=0, concat_axis=0, tiled=True)
    rows_in = lax.all_gather(landed, "wa", axis=0, tiled=True)
    received = rows_in[:, :model_width]
    grad_received = rows_in[:, model_width:]
    w_in, w_out = w_expin[0], w_expout[0]
    pre_act = f32_dot("rd,df->rf", received, w_in)
    activated, gelu_back = jax.vjp(gelu_tanh, pre_act)
    activated_low = low(activated)
    expert_part = f32_dot("rf,fd->rd", activated_low, w_out)
    grad_act = f32_dot("rd,fd->rf", grad_received, w_out)
    grad_pre = low(gelu_back(grad_act)[0])
    grad_inpart = f32_dot("rf,df->rd", grad_pre, w_in)
    rows_out = jnp.concatenate([low(expert_part), low(grad_inpart)], axis=1)
    summed_part = lax.psum_scatter(rows_out, "wa", scatter_dimension=0, tiled=True)
    returned = lax.all_to_all(summed_part, "ctx", split_axis=0, concat_axis=0, tiled=True)
    slot_rows = lax.all_gather(returned, "wa", axis=0, tiled=True)
    grad_wout = f32_dot("rf,rd->fd", activated_low, grad_received)[None]
    grad_win = f32_dot("rd,rf->df", received, grad_pre)[None]
    token_rows = f32_dot("ts,sd->td", combine, slot_rows)
    expert_out = token_rows[:, :model_width]
    grad_from_experts = token_rows[:, model_width:]

    output_rows = hidden1 + gate_value[:, None] * expert_out
    grad_gate = jnp.sum(grad_rows * expert_out, axis=1)
    grad_logits = router_prob * (chosen_float - gate_value[:, None]) * grad_gate[:, None]
    router_float = w_router.astype(jnp.float32)
    grad_normed2 = grad_from_experts + jnp.einsum(
        "te,de->td", grad_logits, router_float, precision=highest
    )
    grad_router = jnp.einsum(
        "td,te->de", normed2_low.astype(jnp.float32), grad_logits, precision=highest
    )
    grad_norm2_in, grad_gain2 = rms_backward(hidden1, scale2, gain_ffn, grad_normed2)
    grad_hidden1 = grad_rows + grad_norm2_in
    grad_attn_low = low(grad_hidden1)
    grad_proj = f32_dot("tk,td->kd", attended_low, grad_attn_low)
    grad_attended = low(f32_dot("td,kd->tk", grad_attn_low, w_proj))
    delta = jnp.sum(
        (grad_attended.astype(jnp.float32) * attended).reshape(tok_count, head_local, head_dim),
        axis=2,
    )
    grad_all = lax.all_gather(with_stats(grad_attended.T, delta.T), "ctx", axis=0)
    early = jnp.concatenate(
        [low(grad_proj), low(grad_router).T, low(grad_gain2)[None, :]], axis=0
    )
    dquery, dline = attend_back(
        base, query_low, grad_attended, attended, lse, kv_all, head_dim
    )
    dkey, dvalue = key_back(base_t, key_low, value_low, query_all, grad_all, head_dim)
    early_sum = lax.psum(early, "ctx")
    folded = sum(jnp.roll(dline[:, row, :], block_len - 1 - row, axis=1) for row in range(8))
    grad_bias = jnp.einsum("bj,hj->bh", in_bucket, folded, precision=highest)
    dquery_low = low(dquery)
    dqkv_low = jnp.concatenate([dquery_low, low(dkey), low(dvalue)], axis=1)
    w_qkv = jnp.concatenate([w_query, w_kv], axis=1)
    grad_wqkv = low(f32_dot("tc,tk->ck", normed1_low, dqkv_low))
    grad_normed1_part = f32_dot("tk,ck->tc", dqkv_low, w_qkv)
    gain_part = jnp.sum(grad_normed1_part * flat_rows * scale1, axis=0)
    small = jnp.concatenate([gain_part, grad_bias.reshape(-1)])
    small = jnp.pad(small, (0, -small.shape[0] % 1024)).reshape(-1, 128)
    small_all = lax.all_gather(small, ("ctx", "wa"), axis=0).reshape(ctx_size, wa_size, -1)
    sum_gain1 = jnp.sum(small_all[:, :, :model_width], axis=(0, 1))
    bias_all = jnp.sum(small_all[:, :, model_width : model_width + grad_bias.size], axis=0)
    sum_bias = lax.dynamic_index_in_dim(bias_all, wa_index, 0, False).reshape(grad_bias.shape)
    grad_normed1 = lax.psum(low(grad_normed1_part), "wa").astype(jnp.float32)
    grad_norm1_in, _ = rms_backward(flat_rows, scale1, gain_attn, grad_normed1)
    grad_inputs = grad_hidden1 + grad_norm1_in

    grad_wqkv, early_sum = lax.optimization_barrier((grad_wqkv, early_sum))
    sum_wqkv = lax.psum(grad_wqkv, "ctx").astype(jnp.float32)
    early_sum = early_sum.astype(jnp.float32)
    return (
        by_position(output_rows),
        by_position(grad_inputs),
        sum_gain1,
        sum_wqkv[:, :head_cols],
        sum_wqkv[:, head_cols : 2 * head_cols],
        sum_wqkv[:, 2 * head_cols :],
        early_sum[:head_cols],
        sum_bias,
        early_sum[head_cols + expert_count],
        early_sum[head_cols : head_cols + expert_count].T,
        grad_win,
        grad_wout,
    )


def solution(mesh):
    in_specs = (
        P("ctx", None, None),
        P("ctx", None, None),
        P(),
        P(None, "wa"),
        P(None, "wa"),
        P(None, "wa"),
        P("wa", None),
        P(None, "wa"),
        P(),
        P(),
        P("ctx", None, "wa"),
        P("ctx", "wa", None),
        P("ctx", None, None),
        P(),
    )
    out_specs = (
        P("ctx", None, None),
        P("ctx", None, None),
        P(),
        P(None, "wa"),
        P(None, "wa"),
        P(None, "wa"),
        P("wa", None),
        P(None, "wa"),
        P(),
        P(),
        P("ctx", None, "wa"),
        P("ctx", "wa", None),
    )
    return jax.shard_map(body, mesh=mesh, in_specs=in_specs, out_specs=out_specs, check_vma=False)
```
